32 devices in a mesh: groups: 2 (over x), row: 16 (over z, y, core).
Axes of the slice: x: 2, y: 2, z: 4, core: 2. Of those that a mesh axis runs over, the one named last changes fastest.
Arguments:
- three_center: bfloat16 [4096, 768], P(('groups', 'row')), parts along dimension 0, may hold values from -4 to 4
- tau_weights: float32 [1536], P('groups'), parts along dimension 0, may hold values from 0.02 to 1
- tile_mask: int32 [16, 6], P('row'), may hold values 0 or 1
- dest: int32 [16, 8], P('row'), may hold values from 0 to 15, all different within a row; in each aligned block of 1 rows (0 to 0, 1 to 1, ...) no two rows name the same one
- metric_half: bfloat16 [2048, 128], P('row'), may hold values from -0.375 to 0.375
Outputs:
- chi_mirror: bfloat16 [32, 8, 128, 128], P(('groups', 'row')), parts along dimension 0
- sandwich: float32 [256, 128], P(('groups', 'row')), parts along dimension 0
The draws below stay inside these ranges and needn't reach their ends.
There are 2 independent parts, one for each index of `groups`. The reference program is written for one: setup_inputs(seed, part) draws one part's arguments, and reference() takes and returns one part's arrays. A program takes and returns all parts, laid end to end along the dimension named above; an argument that names none is the same for every part. Nothing has to cross between parts.
Inputs may be any that keep to these rules, and one draw needn't show every extreme that they name: `dest`: each row names 8 different devices; among the 1 block-rows of one device no device is named twice.
All inputs are finite; a program needn't handle non-finite values. No bound on the sum of `tile_mask` on one device may be relied on, other than what follows from the above.
Results may differ from the reference program's by a relative error of at most 0.0047.
Values may be sent and summed in bfloat16 or wider, within the bound.
No kernel may reach another device: no remote copies, remote signals or barrier semaphores. Data moves between devices by JAX's collectives and lax.ppermute only.
A program may use at most 64 MiB of HBM per device.

```python
import math
import jax
import jax.numpy as jnp
import numpy as np
from jax import lax

BLOCK = 128
NT = 6
BPD = 1
TOP = 8
WC = 128
L = 768
NB = 16
NAUX = 2048
N_ROW = 16


def touch_ends(values, own_key, low, top_value):
    longest = values.shape.index(max(values.shape))
    spots = []
    for shift in (0, 1):
        where = [jax.random.randint(jax.random.fold_in(own_key, axis), (), 0, length) for axis, length in enumerate(values.shape)]
        where[longest] = (where[longest] + shift) % values.shape[longest]
        spots.append(tuple(where))
    return values.at[spots[0]].set(low).at[spots[1]].set(top_value)


def with_spikes(values, rng, source, target, blocks, factor):
    owner, partner = [(jnp.arange(values.shape[position]) // (values.shape[position] // blocks)).reshape([-1 if axis == position else 1 for axis in range(values.ndim)]) for position in (source, target)]
    chosen = jax.random.permutation(rng, blocks)[partner]
    strong = (owner == chosen) | (owner == (partner + blocks // 2) % blocks)
    return jnp.where(strong, factor * values, values)


def block_scale(key, extent, split, smallest, top_value):
    factor_of, own = 1.0, jax.random.fold_in(key, 6)
    for dim, parts in split:
        draws = jnp.exp(jax.random.uniform(jax.random.fold_in(own, dim), (parts,), jnp.float32, smallest / len(split), top_value / len(split)))
        factor_of = factor_of * jnp.repeat(draws, extent[dim] // parts).reshape([-1 if axis == dim else 1 for axis in range(len(extent))])
    return factor_of


def deal_out(rng, own, number, rows, number_of, top, most, skew):
    sequence = jax.random.permutation(rng, number_of)
    crowded, usual = portions_of(number_of, rows * top, most, skew, True), portions_of(number_of, rows * top, most, skew, False)
    places = jnp.arange(number_of)

    def named(lengths, rotation):
        used = int((lengths > 0).sum())
        fixed = max(1, used // 4)
        shifted = fixed + (places - fixed + rotation * (used - fixed)) % max(1, number_of - fixed)
        return jnp.zeros((number_of,), jnp.int32).at[sequence[jnp.where(places < fixed, places, shifted)]].set(jnp.asarray(lengths, jnp.int32))

    lengths = jnp.where(number % 4 == 0, named(crowded, number // 4), named(usual, number - number // 4 - 1))
    mixed = jax.random.permutation(jax.random.fold_in(own, 3), number_of)
    donor, sink = mixed[0:number_of // 2 * 2:2], mixed[1:number_of // 2 * 2:2]
    slack = jnp.minimum(lengths[donor] - 1, most - lengths[sink]) // 2
    slack = jnp.where((donor == sequence[0]) | (sink == sequence[0]) | (lengths[sink] == 0), 0, jnp.maximum(slack, 0))
    shifted = jax.random.randint(jax.random.fold_in(own, 4), (number_of // 2,), 0, 1 << 20) % (slack + 1)
    lengths = lengths.at[donor].add(-shifted).at[sink].add(shifted)
    labels = jnp.searchsorted(jnp.cumsum(lengths), jnp.arange(rows * top), side="right").astype(jnp.int32)
    listing = labels.reshape(top, rows).T
    listing = listing[jax.random.permutation(jax.random.fold_in(own, 1), rows)]
    rotation = jax.random.randint(jax.random.fold_in(own, 2), (rows, 1), 0, top)
    return jnp.take_along_axis(listing, (jnp.arange(top)[None, :] + rotation) % top, axis=1)


def portions_of(count, total, reach, skew, full):
    weights = [(1 << 20) // math.isqrt(rank ** skew) + 1 for rank in range(1, count + 1)]
    largest = reach if full else min(reach, max(-(-total // count), total * weights[0] // sum(weights)))
    least = 1 if total - largest >= count - 1 else 0
    holding, rest = [largest] + [least] * (count - 1), total - largest - least * (count - 1)
    while rest > 0:
        candidates = [i for i in range(1, count) if holding[i] < largest] or [i for i in range(1, count) if holding[i] < reach]
        pool, remaining = sum([weights[i] for i in candidates]), rest
        for i in candidates:
            addition = min(reach - holding[i], max(1, remaining * weights[i] // pool), rest)
            holding[i] = holding[i] + addition
            rest = rest - addition
    return np.array(holding)


def normal_values(own_key, dims, deviation, bound, cuts=(), held_as=jnp.bfloat16):
    result = deviation * jax.random.normal(own_key, dims, jnp.float32)
    if cuts:
        result = result * block_scale(own_key, dims, cuts, -0.22, 0.18)
    return jnp.clip(result, -bound, bound).astype(held_as)


def bell_draw_with(stream_key, dims, deviation, bound, cuts, heavy, dtype=jnp.bfloat16):
    result = deviation * jax.random.normal(stream_key, dims, jnp.float32)
    if cuts:
        result = result * block_scale(stream_key, dims, cuts, -0.22, 0.18)
    return jnp.clip(with_spikes(result, jax.random.fold_in(stream_key, 3), *heavy), -bound, bound).astype(dtype)


def setup_inputs(seed: int = 0, part: int = 0) -> dict:
    keys = jax.random.split(jax.random.key(seed), 6)
    part_splits = jax.random.split(jax.random.fold_in(keys[5], part), 6)
    three_center = normal_values(part_splits[0], (NAUX, L), 0.3, 4.0, ((0, 16),))
    tau_weights = jnp.clip(jnp.exp(jax.random.uniform(part_splits[1], (L,), jnp.float32, math.log(0.02), math.log(1.0))), 0.02, 1.0)
    tile_mask = touch_ends((jax.random.randint(keys[2], (NB, NT), 0, 4) < 3).astype(jnp.int32), jax.random.fold_in(keys[2], 1), 0, 1)
    dest_keys = jax.random.split(jax.random.fold_in(keys[3], 1), NB // BPD)
    dest_turns = jax.random.permutation(jax.random.fold_in(keys[3], 3), NB // BPD)
    dest = jax.vmap(lambda own, number: deal_out(jax.random.fold_in(keys[3], 2), own, number, BPD, N_ROW, TOP, 1, 2))(dest_keys, dest_turns).reshape((NB, TOP))
    metric_half = bell_draw_with(keys[4], (NAUX, WC), (NAUX // 4) ** -0.5, 0.375, ((0, 16),), (0, 1, 16, 2.0))
    return {"three_center": three_center, "tau_weights": tau_weights, "tile_mask": tile_mask, "dest": dest, "metric_half": metric_half}


def reference(three_center, tau_weights, tile_mask, dest, metric_half):
    tiles = L // BLOCK
    width = BPD * BLOCK
    masked = (three_center.reshape(NB, BLOCK, tiles, BLOCK) * tile_mask.astype(jnp.bfloat16)[:, None, :, None]).reshape(NB * BLOCK, L)
    scaled = (masked.astype(jnp.float32) * tau_weights[None, :]).astype(jnp.bfloat16)
    zero = jnp.zeros((), jnp.int32)

    def visit(pair_index, carry):
        mirror, product = carry
        source = (pair_index // TOP).astype(jnp.int32)
        column = (pair_index % TOP).astype(jnp.int32)
        owner = dest[source, column].astype(jnp.int32)
        rows = lax.dynamic_slice_in_dim(masked, source * BLOCK, BLOCK, 0)
        owner_rows = lax.dynamic_slice_in_dim(scaled, owner * width, width, 0)
        block = jnp.dot(rows, owner_rows.T, preferred_element_type=jnp.float32).astype(jnp.bfloat16)
        mirror = lax.dynamic_update_slice(mirror, block[None, None], (source, column, zero, zero))
        metric_rows = lax.dynamic_slice_in_dim(metric_half, source * BLOCK, BLOCK, 0)
        added = jnp.dot(block.T, metric_rows, preferred_element_type=jnp.float32)
        current = lax.dynamic_slice_in_dim(product, owner * width, width, 0)
        product = lax.dynamic_update_slice_in_dim(product, current + added, owner * width, 0)
        return mirror, product

    mirror = jnp.zeros((NB, TOP, BLOCK, width), jnp.bfloat16)
    product = jnp.zeros((NB * BLOCK, WC), jnp.float32)
    mirror, product = lax.fori_loop(jnp.int32(0), jnp.int32(NB * TOP), visit, (mirror, product))
    rounded = product.astype(jnp.bfloat16)
    partial_value = jnp.dot(metric_half.T, rounded, preferred_element_type=jnp.float32)
    return mirror, partial_value + partial_value.T
```

```python
import functools

import jax
import jax.numpy as jnp
from jax import lax
from jax.experimental import pallas as pl
from jax.experimental.pallas import tpu as pltpu
from jax.sharding import PartitionSpec as P

BLOCK = 128
LIST_ROWS = 16
NT_DIMS = (((1,), (1,)), ((), ()))
NN_DIMS = (((1,), (0,)), ((), ()))
TN_DIMS = (((0,), (0,)), ((), ()))


def dot(a, b, dims=NN_DIMS):
    return lax.dot_general(a, b, dims, preferred_element_type=jnp.float32)


def split(x):
    high = x.astype(jnp.bfloat16)
    return high, (x - high.astype(jnp.float32)).astype(jnp.bfloat16)


def pack_kernel(tiles, fanout, mask_ref, dest_ref, rows_ref, tau_ref, metric_ref, out_ref):
    for t in range(tiles):
        cols = slice(t * BLOCK, (t + 1) * BLOCK)
        weight = tau_ref[:, cols] * mask_ref[0, t].astype(jnp.float32)
        out_ref[cols, :] = (rows_ref[:, cols].astype(jnp.float32) * weight).astype(jnp.bfloat16)
    out_ref[tiles * BLOCK : (tiles + 1) * BLOCK, :] = metric_ref[...]
    lane = lax.broadcasted_iota(jnp.int32, (LIST_ROWS, BLOCK), 1)
    listed = jnp.zeros((LIST_ROWS, BLOCK), jnp.float32)
    for j in range(fanout):
        listed += (lane == dest_ref[0, j]).astype(jnp.float32)
    out_ref[(tiles + 1) * BLOCK :, :] = listed.astype(jnp.bfloat16)


def block_kernel(devices, tiles, fanout, *refs):
    me_ref, mask_ref, dest_ref, rows_ref, tau_ref = refs[:5]
    pieces = refs[5 : 5 + devices]
    chi_ref, sand_ref, slot, listed, window = refs[5 + devices :]
    me = me_ref[0]
    window_rows = BLOCK // devices
    depth = tiles * BLOCK

    def init(e, _):
        slot[e] = -1
        return 0

    lax.fori_loop(0, devices, init, 0)
    for j in range(fanout):
        slot[dest_ref[0, j]] = j

    masked = jnp.concatenate(
        [
            rows_ref[:, t * BLOCK : (t + 1) * BLOCK] * mask_ref[0, t].astype(jnp.bfloat16)
            for t in range(tiles)
        ],
        axis=1,
    )

    def scaled_of(ref):
        return jnp.concatenate([ref[t * BLOCK : (t + 1) * BLOCK, :] for t in range(tiles)], axis=1)

    def metric_of(ref):
        return ref[depth : depth + BLOCK, :]

    lane = lax.broadcasted_iota(jnp.int32, (BLOCK, BLOCK), 0)
    column = lax.broadcasted_iota(jnp.int32, (BLOCK, BLOCK), 1)
    pick = (lane == column + me * window_rows).astype(jnp.bfloat16)[:, :window_rows]
    if devices < BLOCK:
        listed[devices:, :] = jnp.zeros((BLOCK - devices, BLOCK), jnp.float32)
    for m in range(devices):
        e = me ^ m
        scaled = scaled_of(pieces[m])
        own = dot(metric_of(pieces[m]), pick).astype(jnp.bfloat16)
        window[m * window_rows : (m + 1) * window_rows, :] = dot(own, scaled, TN_DIMS)
        listed[m : m + 1, :] = pieces[m][depth + BLOCK : depth + BLOCK + 1, :].astype(jnp.float32)
        j = slot[e]

        @pl.when(j >= 0)
        def _(scaled=scaled, j=j):
            chi_ref[0, j] = dot(masked, scaled, NT_DIMS).astype(jnp.bfloat16)

    by_piece = (lane == (column ^ me)).astype(jnp.bfloat16)
    routes = dot(listed[...].astype(jnp.bfloat16), by_piece)
    both = (routes + routes.T).astype(jnp.bfloat16)
    spread = (lane // window_rows == column).astype(jnp.bfloat16)
    pair = dot(dot(spread, both).astype(jnp.bfloat16), spread, NT_DIMS)
    pair = jnp.where(lane % window_rows == column % window_rows, pair, 0.0).astype(jnp.bfloat16)
    high, low = split(window[...])
    mixed = (dot(pair, high) + dot(pair, low)) / tau_ref[...]
    mixed_both = jnp.concatenate(split(mixed), axis=0)
    total = jnp.zeros((BLOCK, BLOCK), jnp.float32)
    for m in range(devices):
        both_parts = dot(scaled_of(pieces[m]), mixed_both, NT_DIMS)
        part = both_parts[:, :BLOCK] + both_parts[:, BLOCK:]
        part = jnp.where(column // window_rows == m, part, 0.0)
        high, low = split(part)
        total += dot(jnp.concatenate([high, low], axis=0), jnp.concatenate([metric_of(pieces[m])] * 2, axis=0), TN_DIMS)
    rows = [total[e * window_rows : (e + 1) * window_rows, :] for e in range(devices)]
    sand_ref[...] = functools.reduce(lambda a, b: a + b, rows)


def body(three_center, tau_weights, tile_mask, dest, metric_half):
    devices = lax.axis_size("row")
    contracted = three_center.shape[1]
    tiles = contracted // BLOCK
    fanout = dest.shape[1]
    window_rows = BLOCK // devices
    piece_rows = (tiles + 1) * BLOCK + LIST_ROWS
    smem = pl.BlockSpec(memory_space=pltpu.SMEM)
    vmem = pl.BlockSpec(memory_space=pltpu.VMEM)
    tau = tau_weights.reshape(1, contracted)
    own = pl.pallas_call(
        functools.partial(pack_kernel, tiles, fanout),
        out_shape=jax.ShapeDtypeStruct((piece_rows, BLOCK), jnp.bfloat16),
        in_specs=[smem, smem, vmem, vmem, vmem],
        out_specs=vmem,
        name="pack",
    )(tile_mask, dest, three_center, tau, metric_half)

    def swap(piece, mask):
        return lax.ppermute(piece, "row", [(i, i ^ mask) for i in range(devices)])

    pieces = {0: own}
    for mask in range(4, devices, 4):
        pieces[mask] = swap(own, mask)
    for mask in range(0, devices, 4):
        pieces[mask + 2] = swap(pieces[mask], 2)
    for mask in range(0, devices, 2):
        pieces[mask + 1] = swap(pieces[mask], 1)
    me = lax.axis_index("row").astype(jnp.int32).reshape(1)
    return pl.pallas_call(
        functools.partial(block_kernel, devices, tiles, fanout),
        out_shape=(
            jax.ShapeDtypeStruct((1, fanout, BLOCK, BLOCK), jnp.bfloat16),
            jax.ShapeDtypeStruct((window_rows, BLOCK), jnp.float32),
        ),
        in_specs=[smem, smem, smem, vmem, vmem] + [vmem] * devices,
        out_specs=(vmem, vmem),
        scratch_shapes=[
            pltpu.SMEM((devices,), jnp.int32),
            pltpu.VMEM((BLOCK, BLOCK), jnp.float32),
            pltpu.VMEM((BLOCK, contracted), jnp.float32),
        ],
        compiler_params=pltpu.CompilerParams(vmem_limit_bytes=40 * 1024 * 1024),
        name="blocks",
    )(me, tile_mask, dest, three_center, tau, *[pieces[m] for m in range(devices)])


def solution(mesh):
    return jax.shard_map(
        body,
        mesh=mesh,
        in_specs=(
            P(("groups", "row"), None),
            P("groups"),
            P("row", None),
            P("row", None),
            P("row", None),
        ),
        out_specs=(P(("groups", "row"), None, None, None), P(("groups", "row"), None)),
        check_vma=False,
    )
```

```python
import functools

import jax
import jax.numpy as jnp
from jax import lax
from jax.experimental import pallas as pl
from jax.experimental.pallas import tpu as pltpu
from jax.sharding import PartitionSpec as P

BLOCK = 128
LIST_ROWS = 16
LAYER = 4
NT_DIMS = (((1,), (1,)), ((), ()))
NN_DIMS = (((1,), (0,)), ((), ()))


def dot(a, b, dims=NN_DIMS):
    return lax.dot_general(a, b, dims, preferred_element_type=jnp.float32)


def split(x):
    high = x.astype(jnp.bfloat16)
    return high, (x - high.astype(jnp.float32)).astype(jnp.bfloat16)


def pack_kernel(mask_ref, dest_ref, rows_ref, tau_ref, metric_ref, piece_ref, masked_ref, row_ref):
    tiles = mask_ref.shape[1]
    depth = tiles * BLOCK
    row_ref[...] = tau_ref[...].reshape(1, depth)
    for t in range(tiles):
        cols = slice(t * BLOCK, (t + 1) * BLOCK)
        kept = rows_ref[:, cols].astype(jnp.float32) * mask_ref[0, t].astype(jnp.float32)
        masked_ref[:, cols] = kept.astype(jnp.bfloat16)
        piece_ref[cols, :] = (kept * row_ref[:, cols]).astype(jnp.bfloat16)
    piece_ref[depth : depth + BLOCK, :] = metric_ref[...]
    lane = lax.broadcasted_iota(jnp.int32, (LIST_ROWS, BLOCK), 1)
    listed = jnp.zeros((LIST_ROWS, BLOCK), jnp.float32)
    for j in range(dest_ref.shape[1]):
        listed += (lane == dest_ref[0, j]).astype(jnp.float32)
    piece_ref[depth + BLOCK :, :] = listed.astype(jnp.bfloat16)


def scaled_of(piece):
    depth = piece.shape[0] - BLOCK - LIST_ROWS
    return jnp.concatenate([piece[t : t + BLOCK, :] for t in range(0, depth, BLOCK)], axis=1)


def metric_of(piece):
    depth = piece.shape[0] - BLOCK - LIST_ROWS
    return piece[depth : depth + BLOCK, :]


def blocks_of(me, masked, pieces, strips, window):
    rows = window.shape[0] // len(pieces)
    lane = lax.broadcasted_iota(jnp.int32, (rows, BLOCK), 1)
    row = lax.broadcasted_iota(jnp.int32, (rows, BLOCK), 0)
    pick = (lane == row + me * rows).astype(jnp.bfloat16)
    own = [dot(pick, metric_of(piece), NT_DIMS).astype(jnp.bfloat16) for piece in pieces]
    for k, piece in enumerate(pieces):
        scaled = scaled_of(piece)
        window[k * rows : (k + 1) * rows, :] = dot(own[k], scaled)
        strips[k] = dot(masked, scaled, NT_DIMS).astype(jnp.bfloat16)


def early_kernel(me_ref, masked_ref, *refs):
    blocks_of(me_ref[0], masked_ref[...], refs[:-2], refs[-2], refs[-1])


def last_kernel(devices, early, me_ref, dest_ref, masked_ref, tau_ref, *refs):
    pieces = refs[:devices]
    early_strips = refs[devices : devices + early]
    early_windows = refs[devices + early : devices + 2 * early]
    chi_ref, sand_ref, strips, window, listed, sems = refs[devices + 2 * early :]
    me = me_ref[0]
    rows = BLOCK // devices
    fanout = dest_ref.shape[1]
    done = 0
    for k in range(early):
        count = early_strips[k].shape[0]
        strips[done : done + count] = early_strips[k][...]
        window[done * rows : (done + count) * rows, :] = early_windows[k][...]
        done += count
    blocks_of(me, masked_ref[...], pieces[done:], strips.at[done:], window.at[done * rows :])
    copies = [
        pltpu.make_async_copy(strips.at[dest_ref[0, j] ^ me], chi_ref.at[0, j], sems.at[j])
        for j in range(fanout)
    ]
    for copy in copies:
        copy.start()

    for m in range(devices):
        entry = pieces[m][pieces[m].shape[0] - LIST_ROWS :, :].astype(jnp.float32)
        listed[m * rows : (m + 1) * rows, :] = entry[:rows, :]
    row = lax.broadcasted_iota(jnp.int32, (BLOCK, BLOCK), 0)
    column = lax.broadcasted_iota(jnp.int32, (BLOCK, BLOCK), 1)
    by_piece = (row == (column // rows ^ me)).astype(jnp.bfloat16)
    routes = dot(listed[...].astype(jnp.bfloat16), by_piece)
    same = row % rows == column % rows
    pair = jnp.where(same, routes + routes.T, 0.0).astype(jnp.bfloat16)
    mixed = dot(jnp.concatenate([pair, pair], axis=1), jnp.concatenate(split(window[...]), axis=0))
    high, low = split(mixed / tau_ref[...])
    sides = []
    for m in range(devices):
        part = slice(m * rows, (m + 1) * rows)
        side = dot(jnp.concatenate([high[part], low[part]], axis=0), scaled_of(pieces[m]), NT_DIMS)
        sides.append(side[:rows] + side[rows:])
    total = jnp.zeros((2 * rows, BLOCK), jnp.float32)
    for m in range(devices):
        total += dot(jnp.concatenate(split(sides[m]), axis=0), metric_of(pieces[m]))
    sand_ref[...] = total[:rows] + total[rows:]
    for copy in copies:
        copy.wait()


def after(value, *others):
    return lax.optimization_barrier((value, *others))[0]


def gather_pieces(own, devices):
    def swap(piece, mask):
        return lax.ppermute(piece, "row", [(i, i ^ mask) for i in range(devices)])

    far = list(range(LAYER, devices, LAYER))
    got = {0: own, 2: swap(own, 2)}
    for mask in far:
        got[mask] = swap(own, mask)
    for k, mask in enumerate(far):
        got[mask + 2] = swap(after(got[mask], *[got[m] for m in far[:k]]), 2)
    got[1] = swap(after(own, got[2]), 1)
    got[3] = swap(got[2], 1)
    for k, mask in enumerate(far):
        later = got[far[k + 1]] if k + 1 < len(far) else got[mask - 2]
        got[mask + 1] = swap(after(got[mask], got[mask - 2]), 1)
        got[mask + 3] = swap(after(got[mask + 2], later), 1)
    return [got[m] for m in range(devices)]


def body(three_center, tau_weights, tile_mask, dest, metric_half):
    devices = lax.axis_size("row")
    local_rows, contracted = three_center.shape
    fanout = dest.shape[1]
    rows = BLOCK // devices
    piece_rows = contracted + BLOCK + LIST_ROWS
    smem = pl.BlockSpec(memory_space=pltpu.SMEM)
    vmem = pl.BlockSpec(memory_space=pltpu.VMEM)
    own, masked, tau = pl.pallas_call(
        pack_kernel,
        out_shape=(
            jax.ShapeDtypeStruct((piece_rows, BLOCK), jnp.bfloat16),
            jax.ShapeDtypeStruct((local_rows, contracted), jnp.bfloat16),
            jax.ShapeDtypeStruct((1, contracted), jnp.float32),
        ),
        in_specs=[smem, smem, vmem, vmem, vmem],
        out_specs=(vmem, vmem, vmem),
        name="pack",
    )(tile_mask, dest, three_center, tau_weights, metric_half)
    pieces = gather_pieces(own, devices)
    me = lax.axis_index("row").astype(jnp.int32).reshape(1)
    strips, windows = [], []
    for first in range(0, devices - LAYER, LAYER):
        strip, window = pl.pallas_call(
            early_kernel,
            out_shape=(
                jax.ShapeDtypeStruct((LAYER, BLOCK, BLOCK), jnp.bfloat16),
                jax.ShapeDtypeStruct((LAYER * rows, contracted), jnp.float32),
            ),
            in_specs=[smem] + [vmem] * (1 + LAYER),
            out_specs=(vmem, vmem),
            name="early",
        )(me, masked, *pieces[first : first + LAYER])
        strips.append(strip)
        windows.append(window)
    return pl.pallas_call(
        functools.partial(last_kernel, devices, len(strips)),
        out_shape=(
            jax.ShapeDtypeStruct((1, fanout, BLOCK, BLOCK), jnp.bfloat16),
            jax.ShapeDtypeStruct((rows, BLOCK), jnp.float32),
        ),
        in_specs=[smem, smem] + [vmem] * (2 + devices + 2 * len(strips)),
        out_specs=(pl.BlockSpec(memory_space=pl.ANY), vmem),
        scratch_shapes=[
            pltpu.VMEM((devices, BLOCK, BLOCK), jnp.bfloat16),
            pltpu.VMEM((BLOCK, contracted), jnp.float32),
            pltpu.VMEM((BLOCK, BLOCK), jnp.float32),
            pltpu.SemaphoreType.DMA((fanout,)),
        ],
        compiler_params=pltpu.CompilerParams(vmem_limit_bytes=40 * 1024 * 1024),
        name="last",
    )(me, dest, masked, tau, *pieces, *strips, *windows)


def solution(mesh):
    return jax.shard_map(
        body,
        mesh=mesh,
        in_specs=(
            P(("groups", "row"), None),
            P("groups"),
            P("row", None),
            P("row", None),
            P("row", None),
        ),
        out_specs=(P(("groups", "row"), None, None, None), P(("groups", "row"), None)),
        check_vma=False,
    )
```

```python
import functools

import jax
import jax.numpy as jnp
from jax import lax
from jax.experimental import pallas as pl
from jax.experimental.pallas import tpu as pltpu
from jax.sharding import PartitionSpec as P

BLOCK = 128
LIST_ROWS = 16
LAYER = 4
MIB = 1 << 20
NT_DIMS = (((1,), (1,)), ((), ()))
NN_DIMS = (((1,), (0,)), ((), ()))


def dot(a, b, dims=NN_DIMS):
    return lax.dot_general(a, b, dims, preferred_element_type=jnp.float32)


def split(x):
    high = x.astype(jnp.bfloat16)
    return high, (x - high.astype(jnp.float32)).astype(jnp.bfloat16)


def pack_kernel(
    mask_hbm, dest_hbm, rows_hbm, tau_hbm, metric_hbm, piece_ref, mask_ref, dest_ref, rows_ref, tau_ref, sems
):
    tiles = mask_ref.shape[1]
    depth = tiles * BLOCK
    moves = [
        (rows_hbm, rows_ref),
        (tau_hbm, tau_ref),
        (mask_hbm, mask_ref),
        (dest_hbm, dest_ref),
        (metric_hbm, piece_ref.at[depth : depth + BLOCK]),
    ]
    copies = [pltpu.make_async_copy(source, target, sems.at[k]) for k, (source, target) in enumerate(moves)]
    for copy in copies:
        copy.start()
    for copy in copies:
        copy.wait()
    tau = tau_ref[...].reshape(1, depth)
    for t in range(tiles):
        cols = slice(t * BLOCK, (t + 1) * BLOCK)
        weight = tau[:, cols] * mask_ref[0, t].astype(jnp.float32)
        piece_ref[cols, :] = (rows_ref[:, cols].astype(jnp.float32) * weight).astype(jnp.bfloat16)
    lane = lax.broadcasted_iota(jnp.int32, (LIST_ROWS, BLOCK), 1)
    listed = jnp.zeros((LIST_ROWS, BLOCK), jnp.float32)
    for j in range(dest_ref.shape[1]):
        listed += (lane == dest_ref[0, j]).astype(jnp.float32)
    piece_ref[depth + BLOCK :, :] = listed.astype(jnp.bfloat16)


def local_kernel(mask_ref, rows_ref, tau_ref, masked_ref, row_ref):
    row_ref[...] = tau_ref[...].reshape(row_ref.shape)
    for t in range(mask_ref.shape[1]):
        cols = slice(t * BLOCK, (t + 1) * BLOCK)
        masked_ref[:, cols] = rows_ref[:, cols] * mask_ref[0, t].astype(jnp.bfloat16)


def scaled_of(piece):
    depth = piece.shape[0] - BLOCK - LIST_ROWS
    return jnp.concatenate([piece[t : t + BLOCK, :] for t in range(0, depth, BLOCK)], axis=1)


def metric_of(piece):
    depth = piece.shape[0] - BLOCK - LIST_ROWS
    return piece[depth : depth + BLOCK, :]


def blocks_of(me, masked, pieces, strips, windows):
    rows = windows[0].shape[0]
    lane = lax.broadcasted_iota(jnp.int32, (rows, BLOCK), 1)
    row = lax.broadcasted_iota(jnp.int32, (rows, BLOCK), 0)
    pick = (lane == row + me * rows).astype(jnp.bfloat16)
    own = [dot(pick, metric_of(piece), NT_DIMS).astype(jnp.bfloat16) for piece in pieces]
    for k, piece in enumerate(pieces):
        scaled = scaled_of(piece)
        windows[k][...] = dot(own[k], scaled)
        strips[k][...] = dot(masked, scaled, NT_DIMS).astype(jnp.bfloat16)


def early_kernel(me_ref, masked_ref, *refs):
    strips, windows = refs[-2:]
    count = strips.shape[0]
    blocks_of(
        me_ref[0],
        masked_ref[...],
        refs[:-2],
        [strips.at[k] for k in range(count)],
        [windows.at[k] for k in range(count)],
    )


def last_kernel(devices, groups, me_ref, dest_hbm, masked_ref, tau_ref, *refs):
    pieces = refs[:devices]
    early = refs[devices : devices + 2 * len(groups)]
    chi_ref, sand_ref, strips, window, listed, dest_ref, sems, dest_sem = refs[devices + 2 * len(groups) :]
    fetch = pltpu.make_async_copy(dest_hbm, dest_ref, dest_sem)
    fetch.start()
    me = me_ref[0]
    rows = BLOCK // devices
    fanout = dest_ref.shape[1]
    late = [m for m in range(devices) if all(m not in group for group in groups)]
    blocks_of(
        me,
        masked_ref[...],
        [pieces[m] for m in late],
        [strips.at[m] for m in late],
        [window.at[m * rows : (m + 1) * rows] for m in late],
    )
    for group, strip, part in zip(groups, early[::2], early[1::2]):
        for k, m in enumerate(group):
            strips[m] = strip[k]
            window[m * rows : (m + 1) * rows, :] = part[k]
    fetch.wait()
    copies = [
        pltpu.make_async_copy(strips.at[dest_ref[0, j] ^ me], chi_ref.at[0, j], sems.at[j])
        for j in range(fanout)
    ]
    for copy in copies:
        copy.start()

    for m in range(devices):
        entry = pieces[m][pieces[m].shape[0] - LIST_ROWS :, :].astype(jnp.float32)
        listed[m * rows : (m + 1) * rows, :] = entry[:rows, :]
    row = lax.broadcasted_iota(jnp.int32, (BLOCK, BLOCK), 0)
    column = lax.broadcasted_iota(jnp.int32, (BLOCK, BLOCK), 1)
    by_piece = (row == (column // rows ^ me)).astype(jnp.bfloat16)
    routes = dot(listed[...].astype(jnp.bfloat16), by_piece)
    same = row % rows == column % rows
    pair = jnp.where(same, routes + routes.T, 0.0).astype(jnp.bfloat16)
    mixed = dot(jnp.concatenate([pair, pair], axis=1), jnp.concatenate(split(window[...]), axis=0))
    high, low = split(mixed / tau_ref[...])
    sides = []
    for m in range(devices):
        part = slice(m * rows, (m + 1) * rows)
        side = dot(jnp.concatenate([high[part], low[part]], axis=0), scaled_of(pieces[m]), NT_DIMS)
        sides.append(side[:rows] + side[rows:])
    total = jnp.zeros((2 * rows, BLOCK), jnp.float32)
    for m in range(devices):
        total += dot(jnp.concatenate(split(sides[m]), axis=0), metric_of(pieces[m]))
    sand_ref[...] = total[:rows] + total[rows:]
    for copy in copies:
        copy.wait()


def after(value, *others):
    return lax.optimization_barrier((value, others))[0]


def body(three_center, tau_weights, tile_mask, dest, metric_half):
    devices = lax.axis_size("row")
    local_rows, contracted = three_center.shape
    fanout = dest.shape[1]
    rows = BLOCK // devices
    piece_rows = contracted + BLOCK + LIST_ROWS
    smem = pl.BlockSpec(memory_space=pltpu.SMEM)
    vmem = pl.BlockSpec(memory_space=pltpu.VMEM)
    hbm = pl.BlockSpec(memory_space=pltpu.HBM)
    own = pl.pallas_call(
        pack_kernel,
        out_shape=jax.ShapeDtypeStruct((piece_rows, BLOCK), jnp.bfloat16),
        in_specs=[hbm] * 5,
        out_specs=vmem,
        scratch_shapes=[
            pltpu.SMEM(tile_mask.shape, jnp.int32),
            pltpu.SMEM(dest.shape, jnp.int32),
            pltpu.VMEM(three_center.shape, jnp.bfloat16),
            pltpu.VMEM(tau_weights.shape, jnp.float32),
            pltpu.SemaphoreType.DMA((5,)),
        ],
        compiler_params=pltpu.CompilerParams(vmem_limit_bytes=56 * MIB),
        cost_estimate=pl.CostEstimate(flops=0, bytes_accessed=MIB, transcendentals=0),
        name="pack",
    )(tile_mask, dest, three_center, tau_weights, metric_half)
    masked, tau = pl.pallas_call(
        local_kernel,
        out_shape=(
            jax.ShapeDtypeStruct((local_rows, contracted), jnp.bfloat16),
            jax.ShapeDtypeStruct((1, contracted), jnp.float32),
        ),
        in_specs=[smem, vmem, vmem],
        out_specs=(vmem, vmem),
        compiler_params=pltpu.CompilerParams(vmem_limit_bytes=4 * MIB),
        cost_estimate=pl.CostEstimate(flops=0, bytes_accessed=MIB, transcendentals=0),
        name="local",
    )(*after((tile_mask, three_center, tau_weights), own))
    me = lax.axis_index("row").astype(jnp.int32).reshape(1)

    def early(group):
        return pl.pallas_call(
            early_kernel,
            out_shape=(
                jax.ShapeDtypeStruct((len(group), BLOCK, BLOCK), jnp.bfloat16),
                jax.ShapeDtypeStruct((len(group), rows, contracted), jnp.float32),
            ),
            in_specs=[smem] + [vmem] * (1 + len(group)),
            out_specs=(vmem, vmem),
            compiler_params=pltpu.CompilerParams(vmem_limit_bytes=8 * MIB),
            cost_estimate=pl.CostEstimate(flops=0, bytes_accessed=MIB, transcendentals=0),
            name="early",
        )(me, masked, *[got[m] for m in group])

    def swap(piece, mask):
        return lax.ppermute(piece, "row", [(i, i ^ mask) for i in range(devices)])

    far = list(range(LAYER, devices, LAYER))
    near, last = far[0], far[-1]
    got = {0: own}
    for mask in far[1:-1] + [near]:
        got[mask] = swap(own, mask)
    got[2], got[near + 2], got[1] = swap(own, 2), swap(own, near + 2), swap(own, 1)
    got[last] = swap(after(own, got[near], got[1]), last)
    for mask in far[1:-1]:
        got[mask + 2] = swap(after(got[mask], got[near]), 2)
    got[last + 2] = swap(after(got[last], got[near + 2], [got[m + 2] for m in far[1:-1]]), 2)
    got[3] = swap(after(got[2], got[near]), 1)
    for mask in far[:-1]:
        got[mask + 1] = swap(after(got[mask], got[far[1]]), 1)
    got[near + 3] = swap(after(got[near + 2], got[far[1]]), 1)
    for mask in far[1:-1]:
        got[mask + 3] = swap(after(got[mask + 2], got[last]), 1)
    got[last + 1] = swap(after(got[last], [got[m + 2] for m in far[1:-1]]), 1)
    forwarded = [mask + 2 for mask in far[1:-1]]
    first = [m for m in range(last) if m not in forwarded and m - 1 not in forwarded]
    second = [m for m in range(last + 2) if m not in first]
    groups = [first, second]
    masked, tau = after((masked, tau), got[last])
    results = [early(first), early(second)]
    got[last + 3] = swap(after(got[last + 2], results), 1)
    pieces = [got[m] for m in range(devices)]
    return pl.pallas_call(
        functools.partial(last_kernel, devices, groups),
        out_shape=(
            jax.ShapeDtypeStruct((1, fanout, BLOCK, BLOCK), jnp.bfloat16),
            jax.ShapeDtypeStruct((rows, BLOCK), jnp.float32),
        ),
        in_specs=[smem, hbm] + [vmem] * (2 + devices + 2 * len(groups)),
        out_specs=(hbm, vmem),
        scratch_shapes=[
            pltpu.VMEM((devices, BLOCK, BLOCK), jnp.bfloat16),
            pltpu.VMEM((BLOCK, contracted), jnp.float32),
            pltpu.VMEM((BLOCK, BLOCK), jnp.float32),
            pltpu.SMEM(dest.shape, jnp.int32),
            pltpu.SemaphoreType.DMA((fanout,)),
            pltpu.SemaphoreType.DMA,
        ],
        compiler_params=pltpu.CompilerParams(vmem_limit_bytes=24 * MIB),
        cost_estimate=pl.CostEstimate(flops=0, bytes_accessed=MIB, transcendentals=0),
        name="last",
    )(me, dest, masked, tau, *pieces, *[part for result in results for part in result])


def solution(mesh):
    return jax.shard_map(
        body,
        mesh=mesh,
        in_specs=(
            P(("groups", "row"), None),
            P("groups"),
            P("row", None),
            P("row", None),
            P("row", None),
        ),
        out_specs=(P(("groups", "row"), None, None, None), P(("groups", "row"), None)),
        check_vma=False,
    )
```

```python
import functools

import jax
import jax.numpy as jnp
from jax import lax
from jax.experimental import pallas as pl
from jax.experimental.pallas import tpu as pltpu
from jax.sharding import PartitionSpec as P

BLOCK = 128
LIST_ROWS = 16
LAYER = 4
MIB = 1 << 20
NT_DIMS = (((1,), (1,)), ((), ()))
NN_DIMS = (((1,), (0,)), ((), ()))


def dot(a, b, dims=NN_DIMS):
    return lax.dot_general(a, b, dims, preferred_element_type=jnp.float32)


def split(x):
    high = x.astype(jnp.bfloat16)
    return high, (x - high.astype(jnp.float32)).astype(jnp.bfloat16)


def pack_kernel(
    mask_hbm, dest_hbm, rows_hbm, tau_hbm, metric_hbm, piece_ref, mask_ref, dest_ref, rows_ref, tau_ref, sems
):
    tiles = mask_ref.shape[1]
    depth = tiles * BLOCK
    moves = [
        (rows_hbm, rows_ref),
        (tau_hbm, tau_ref),
        (mask_hbm, mask_ref),
        (dest_hbm, dest_ref),
        (metric_hbm, piece_ref.at[depth : depth + BLOCK]),
    ]
    copies = [pltpu.make_async_copy(source, target, sems.at[k]) for k, (source, target) in enumerate(moves)]
    for copy in copies:
        copy.start()
    for copy in copies:
        copy.wait()
    tau = tau_ref[...].reshape(1, depth)
    for t in range(tiles):
        cols = slice(t * BLOCK, (t + 1) * BLOCK)
        weight = tau[:, cols] * mask_ref[0, t].astype(jnp.float32)
        piece_ref[cols, :] = (rows_ref[:, cols].astype(jnp.float32) * weight).astype(jnp.bfloat16)
    lane = lax.broadcasted_iota(jnp.int32, (LIST_ROWS, BLOCK), 1)
    listed = jnp.zeros((LIST_ROWS, BLOCK), jnp.float32)
    for j in range(dest_ref.shape[1]):
        listed += (lane == dest_ref[0, j]).astype(jnp.float32)
    piece_ref[depth + BLOCK :, :] = listed.astype(jnp.bfloat16)


def local_kernel(mask_ref, rows_ref, tau_ref, masked_ref, row_ref):
    row_ref[...] = tau_ref[...].reshape(row_ref.shape)
    for t in range(mask_ref.shape[1]):
        cols = slice(t * BLOCK, (t + 1) * BLOCK)
        masked_ref[:, cols] = rows_ref[:, cols] * mask_ref[0, t].astype(jnp.bfloat16)


def scaled_of(piece):
    depth = piece.shape[0] - BLOCK - LIST_ROWS
    return jnp.concatenate([piece[t : t + BLOCK, :] for t in range(0, depth, BLOCK)], axis=1)


def metric_of(piece):
    depth = piece.shape[0] - BLOCK - LIST_ROWS
    return piece[depth : depth + BLOCK, :]


def blocks_of(me, masked, pieces, strips, windows):
    rows = windows[0].shape[0]
    lane = lax.broadcasted_iota(jnp.int32, (rows, BLOCK), 1)
    row = lax.broadcasted_iota(jnp.int32, (rows, BLOCK), 0)
    pick = (lane == row + me * rows).astype(jnp.bfloat16)
    own = [dot(pick, metric_of(piece), NT_DIMS).astype(jnp.bfloat16) for piece in pieces]
    for k, piece in enumerate(pieces):
        scaled = scaled_of(piece)
        windows[k][...] = dot(own[k], scaled)
        strips[k][...] = dot(masked, scaled, NT_DIMS).astype(jnp.bfloat16)


def early_kernel(me_ref, masked_ref, *refs):
    strips, windows = refs[-2:]
    count = strips.shape[0]
    blocks_of(
        me_ref[0],
        masked_ref[...],
        refs[:-2],
        [strips.at[k] for k in range(count)],
        [windows.at[k] for k in range(count)],
    )


def last_kernel(devices, groups, me_ref, dest_hbm, masked_ref, tau_ref, *refs):
    pieces = refs[:devices]
    early = refs[devices : devices + 2 * len(groups)]
    chi_ref, sand_ref, strips, window, listed, dest_ref, sems, dest_sem = refs[devices + 2 * len(groups) :]
    fetch = pltpu.make_async_copy(dest_hbm, dest_ref, dest_sem)
    fetch.start()
    me = me_ref[0]
    rows = BLOCK // devices
    fanout = dest_ref.shape[1]
    late = [m for m in range(devices) if all(m not in group for group in groups)]
    blocks_of(
        me,
        masked_ref[...],
        [pieces[m] for m in late],
        [strips.at[m] for m in late],
        [window.at[m * rows : (m + 1) * rows] for m in late],
    )
    for group, strip, part in zip(groups, early[::2], early[1::2]):
        for k, m in enumerate(group):
            strips[m] = strip[k]
            window[m * rows : (m + 1) * rows, :] = part[k]
    fetch.wait()
    copies = [
        pltpu.make_async_copy(strips.at[dest_ref[0, j] ^ me], chi_ref.at[0, j], sems.at[j])
        for j in range(fanout)
    ]
    for copy in copies:
        copy.start()

    for m in range(devices):
        entry = pieces[m][pieces[m].shape[0] - LIST_ROWS :, :].astype(jnp.float32)
        listed[m * rows : (m + 1) * rows, :] = entry[:rows, :]
    row = lax.broadcasted_iota(jnp.int32, (BLOCK, BLOCK), 0)
    column = lax.broadcasted_iota(jnp.int32, (BLOCK, BLOCK), 1)
    by_piece = (row == (column // rows ^ me)).astype(jnp.bfloat16)
    routes = dot(listed[...].astype(jnp.bfloat16), by_piece)
    same = row % rows == column % rows
    pair = jnp.where(same, routes + routes.T, 0.0).astype(jnp.bfloat16)
    mixed = dot(jnp.concatenate([pair, pair], axis=1), jnp.concatenate(split(window[...]), axis=0))
    high, low = split(mixed / tau_ref[...])
    sides = []
    for m in range(devices):
        part = slice(m * rows, (m + 1) * rows)
        side = dot(jnp.concatenate([high[part], low[part]], axis=0), scaled_of(pieces[m]), NT_DIMS)
        sides.append(side[:rows] + side[rows:])
    total = jnp.zeros((2 * rows, BLOCK), jnp.float32)
    for m in range(devices):
        total += dot(jnp.concatenate(split(sides[m]), axis=0), metric_of(pieces[m]))
    sand_ref[...] = total[:rows] + total[rows:]
    for copy in copies:
        copy.wait()


def after(value, *others):
    return lax.optimization_barrier((value, others))[0]


def body(three_center, tau_weights, tile_mask, dest, metric_half):
    devices = lax.axis_size("row")
    local_rows, contracted = three_center.shape
    fanout = dest.shape[1]
    rows = BLOCK // devices
    piece_rows = contracted + BLOCK + LIST_ROWS
    smem = pl.BlockSpec(memory_space=pltpu.SMEM)
    vmem = pl.BlockSpec(memory_space=pltpu.VMEM)
    hbm = pl.BlockSpec(memory_space=pltpu.HBM)
    own = pl.pallas_call(
        pack_kernel,
        out_shape=jax.ShapeDtypeStruct((piece_rows, BLOCK), jnp.bfloat16),
        in_specs=[hbm] * 5,
        out_specs=vmem,
        scratch_shapes=[
            pltpu.SMEM(tile_mask.shape, jnp.int32),
            pltpu.SMEM(dest.shape, jnp.int32),
            pltpu.VMEM(three_center.shape, jnp.bfloat16),
            pltpu.VMEM(tau_weights.shape, jnp.float32),
            pltpu.SemaphoreType.DMA((5,)),
        ],
        compiler_params=pltpu.CompilerParams(vmem_limit_bytes=56 * MIB),
        cost_estimate=pl.CostEstimate(flops=0, bytes_accessed=MIB, transcendentals=0),
        name="pack",
    )(tile_mask, dest, three_center, tau_weights, metric_half)
    masked, tau = pl.pallas_call(
        local_kernel,
        out_shape=(
            jax.ShapeDtypeStruct((local_rows, contracted), jnp.bfloat16),
            jax.ShapeDtypeStruct((1, contracted), jnp.float32),
        ),
        in_specs=[smem, vmem, vmem],
        out_specs=(vmem, vmem),
        compiler_params=pltpu.CompilerParams(vmem_limit_bytes=4 * MIB),
        cost_estimate=pl.CostEstimate(flops=0, bytes_accessed=MIB, transcendentals=0),
        name="local",
    )(*after((tile_mask, three_center, tau_weights), own))
    me = lax.axis_index("row").astype(jnp.int32).reshape(1)

    def early(group):
        return pl.pallas_call(
            early_kernel,
            out_shape=(
                jax.ShapeDtypeStruct((len(group), BLOCK, BLOCK), jnp.bfloat16),
                jax.ShapeDtypeStruct((len(group), rows, contracted), jnp.float32),
            ),
            in_specs=[smem] + [vmem] * (1 + len(group)),
            out_specs=(vmem, vmem),
            compiler_params=pltpu.CompilerParams(vmem_limit_bytes=8 * MIB),
            cost_estimate=pl.CostEstimate(flops=0, bytes_accessed=MIB, transcendentals=0),
            name="early",
        )(me, masked, *[got[m] for m in group])

    def swap(piece, mask):
        return lax.ppermute(piece, "row", [(i, i ^ mask) for i in range(devices)])

    far = list(range(LAYER, devices, LAYER))
    near, last = far[0], far[-1]
    got = {0: own}
    for mask in far[1:-1] + [near]:
        got[mask] = swap(own, mask)
    got[2], got[near + 2], got[1] = swap(own, 2), swap(own, near + 2), swap(own, 1)
    if len(far) == 3:
        layer = me[0] // LAYER
        middle = (layer == 1) | (layer == 2)
        onward = (2, 0, 3, 1)
        got[last] = lax.ppermute(
            jnp.where(middle, got[2 * LAYER], got[near]),
            "row",
            [(i, onward[i // LAYER] * LAYER + i % LAYER) for i in range(devices)],
        )
    else:
        got[last] = swap(own, last)
    for mask in far[1:-1]:
        got[mask + 2] = swap(after(got[mask], got[near]), 2)
    got[3] = swap(after(got[2], got[near]), 1)
    first = [0, 1, 2, 3] + far[:-1] + [near + 2]
    groups = [first]
    results = [early(first)]
    got[last + 2] = swap(after(got[last], results[0]), 2)
    got[near + 3] = swap(after(got[near + 2], results[0]), 1)
    for mask in far[1:-1]:
        got[mask + 3] = swap(after(got[mask + 2], results[0]), 1)
    for mask in far:
        got[mask + 1] = swap(after(got[mask], results[0]), 1)
    got[last + 3] = swap(after(got[last + 2], results), 1)
    pieces = [got[m] for m in range(devices)]
    return pl.pallas_call(
        functools.partial(last_kernel, devices, groups),
        out_shape=(
            jax.ShapeDtypeStruct((1, fanout, BLOCK, BLOCK), jnp.bfloat16),
            jax.ShapeDtypeStruct((rows, BLOCK), jnp.float32),
        ),
        in_specs=[smem, hbm] + [vmem] * (2 + devices + 2 * len(groups)),
        out_specs=(hbm, vmem),
        scratch_shapes=[
            pltpu.VMEM((devices, BLOCK, BLOCK), jnp.bfloat16),
            pltpu.VMEM((BLOCK, contracted), jnp.float32),
            pltpu.VMEM((BLOCK, BLOCK), jnp.float32),
            pltpu.SMEM(dest.shape, jnp.int32),
            pltpu.SemaphoreType.DMA((fanout,)),
            pltpu.SemaphoreType.DMA,
        ],
        compiler_params=pltpu.CompilerParams(vmem_limit_bytes=24 * MIB),
        cost_estimate=pl.CostEstimate(flops=0, bytes_accessed=MIB, transcendentals=0),
        name="last",
    )(me, dest, masked, tau, *pieces, *[part for result in results for part in result])


def solution(mesh):
    return jax.shard_map(
        body,
        mesh=mesh,
        in_specs=(
            P(("groups", "row"), None),
            P("groups"),
            P("row", None),
            P("row", None),
            P("row", None),
        ),
        out_specs=(P(("groups", "row"), None, None, None), P(("groups", "row"), None)),
        check_vma=False,
    )
```

```python
import functools

import jax
import jax.numpy as jnp
from jax import lax
from jax.experimental import pallas as pl
from jax.experimental.pallas import tpu as pltpu
from jax.sharding import PartitionSpec as P

BLOCK = 128
LIST_ROWS = 16
LAYER = 4
CUT = 4 * BLOCK
MIB = 1 << 20
NT_DIMS = (((1,), (1,)), ((), ()))
NN_DIMS = (((1,), (0,)), ((), ()))
TN_DIMS = (((0,), (0,)), ((), ()))


def dot(a, b, dims=NN_DIMS):
    return lax.dot_general(a, b, dims, preferred_element_type=jnp.float32)


def split(x):
    high = x.astype(jnp.bfloat16)
    return high, (x - high.astype(jnp.float32)).astype(jnp.bfloat16)


def pack_kernel(
    mask_hbm, dest_hbm, rows_hbm, tau_hbm, metric_hbm, piece_ref, mask_ref, dest_ref, rows_ref, tau_ref, sems
):
    tiles = mask_ref.shape[1]
    depth = tiles * BLOCK
    moves = [
        (rows_hbm, rows_ref),
        (tau_hbm, tau_ref),
        (mask_hbm, mask_ref),
        (dest_hbm, dest_ref),
        (metric_hbm, piece_ref.at[depth : depth + BLOCK]),
    ]
    copies = [pltpu.make_async_copy(source, target, sems.at[k]) for k, (source, target) in enumerate(moves)]
    for copy in copies:
        copy.start()
    for copy in copies:
        copy.wait()
    tau = tau_ref[...].reshape(1, depth)
    for t in range(tiles):
        cols = slice(t * BLOCK, (t + 1) * BLOCK)
        weight = tau[:, cols] * mask_ref[0, t].astype(jnp.float32)
        piece_ref[cols, :] = (rows_ref[:, cols].astype(jnp.float32) * weight).astype(jnp.bfloat16)
    lane = lax.broadcasted_iota(jnp.int32, (LIST_ROWS, BLOCK), 1)
    listed = jnp.zeros((LIST_ROWS, BLOCK), jnp.float32)
    for j in range(dest_ref.shape[1]):
        listed += (lane == dest_ref[0, j]).astype(jnp.float32)
    piece_ref[depth + BLOCK :, :] = listed.astype(jnp.bfloat16)


def local_kernel(mask_ref, rows_ref, tau_ref, masked_ref, row_ref):
    row_ref[...] = tau_ref[...].reshape(row_ref.shape)
    for t in range(mask_ref.shape[1]):
        cols = slice(t * BLOCK, (t + 1) * BLOCK)
        masked_ref[:, cols] = rows_ref[:, cols] * mask_ref[0, t].astype(jnp.bfloat16)


def rows_of(piece, first, count):
    for part in piece:
        if first < part.shape[0]:
            return part[first : first + count, :]
        first -= part.shape[0]


def scaled_of(piece):
    depth = sum(part.shape[0] for part in piece) - BLOCK - LIST_ROWS
    return jnp.concatenate([rows_of(piece, t, BLOCK) for t in range(0, depth, BLOCK)], axis=1)


def metric_of(piece):
    depth = sum(part.shape[0] for part in piece) - BLOCK - LIST_ROWS
    return rows_of(piece, depth, BLOCK)


def listed_of(piece):
    part = piece[-1]
    return part[part.shape[0] - LIST_ROWS :, :]


def grouped(refs, parts):
    pieces = []
    for count in parts:
        pieces.append(tuple(refs[:count]))
        refs = refs[count:]
    return pieces


def strips_of(masked, pieces, strips):
    for k, piece in enumerate(pieces):
        strips[k][...] = dot(masked, scaled_of(piece), NT_DIMS).astype(jnp.bfloat16)


def window_of(me, pieces, windows, grams):
    rows = windows[0].shape[0]
    lane = lax.broadcasted_iota(jnp.int32, (rows, BLOCK), 1)
    row = lax.broadcasted_iota(jnp.int32, (rows, BLOCK), 0)
    pick = (lane == row + me * rows).astype(jnp.bfloat16)
    own = [dot(pick, metric_of(piece), NT_DIMS).astype(jnp.bfloat16) for piece in pieces]
    for k, piece in enumerate(pieces):
        windows[k][...] = dot(own[k], scaled_of(piece))
    for k, piece in enumerate(pieces):
        grams[k][...] = dot(scaled_of(piece), metric_of(piece), TN_DIMS).astype(jnp.bfloat16)


def early_kernel(parts, masked_ref, *refs):
    strips, windows, grams = refs[-3:]
    pieces = grouped(refs[:-3], parts)
    each = range(len(pieces))
    strips_of(masked_ref[...], pieces, [strips.at[k] for k in each])
    window_of(lax.axis_index("row"), pieces, [windows.at[k] for k in each], [grams.at[k] for k in each])


def last_kernel(devices, groups, parts, dest_hbm, masked_ref, tau_ref, *refs):
    pieces = grouped(refs, parts)
    early = refs[sum(parts) : sum(parts) + 3 * len(groups)]
    chi_ref, sand_ref, strips, window, late_grams, listed, dest_ref, sems, dest_sem = refs[
        sum(parts) + 3 * len(groups) :
    ]
    fetch = pltpu.make_async_copy(dest_hbm, dest_ref, dest_sem)
    fetch.start()
    me = lax.axis_index("row")
    rows = BLOCK // devices
    fanout = dest_ref.shape[1]
    late = [m for m in range(devices) if all(m not in group for group in groups)]
    strips_of(masked_ref[...], [pieces[m] for m in late], [strips.at[m] for m in late])
    grams = {m: late_grams.at[k] for k, m in enumerate(late)}
    for group, strip, part, gram in zip(groups, early[::3], early[1::3], early[2::3]):
        for k, m in enumerate(group):
            strips[m] = strip[k]
            window[m * rows : (m + 1) * rows, :] = part[k]
            grams[m] = gram.at[k]
    fetch.wait()
    copies = [
        pltpu.make_async_copy(strips.at[dest_ref[0, j] ^ me], chi_ref.at[0, j], sems.at[j])
        for j in range(fanout)
    ]
    for copy in copies:
        copy.start()
    window_of(
        me,
        [pieces[m] for m in late],
        [window.at[m * rows : (m + 1) * rows] for m in late],
        [grams[m] for m in late],
    )

    for m in range(devices):
        entry = listed_of(pieces[m]).astype(jnp.float32)
        listed[m * rows : (m + 1) * rows, :] = entry[:rows, :]
    row = lax.broadcasted_iota(jnp.int32, (BLOCK, BLOCK), 0)
    column = lax.broadcasted_iota(jnp.int32, (BLOCK, BLOCK), 1)
    by_piece = (row == (column // rows ^ me)).astype(jnp.bfloat16)
    routes = dot(listed[...].astype(jnp.bfloat16), by_piece)
    same = row % rows == column % rows
    pair = jnp.where(same, routes + routes.T, 0.0).astype(jnp.bfloat16)
    mixed = dot(jnp.concatenate([pair, pair], axis=1), jnp.concatenate(split(window[...]), axis=0))
    high, low = split(mixed / tau_ref[...])
    total = jnp.zeros((2 * rows, BLOCK), jnp.float32)
    for m in range(devices):
        part = slice(m * rows, (m + 1) * rows)
        total += dot(jnp.concatenate([high[part], low[part]], axis=0), grams[m][...])
    sand_ref[...] = total[:rows] + total[rows:]
    for copy in copies:
        copy.wait()


def after(value, *others):
    return lax.optimization_barrier((value, others))[0]


def body(three_center, tau_weights, tile_mask, dest, metric_half):
    devices = lax.axis_size("row")
    local_rows, contracted = three_center.shape
    fanout = dest.shape[1]
    rows = BLOCK // devices
    piece_rows = contracted + BLOCK + LIST_ROWS
    smem = pl.BlockSpec(memory_space=pltpu.SMEM)
    vmem = pl.BlockSpec(memory_space=pltpu.VMEM)
    hbm = pl.BlockSpec(memory_space=pltpu.HBM)
    own = pl.pallas_call(
        pack_kernel,
        out_shape=jax.ShapeDtypeStruct((piece_rows, BLOCK), jnp.bfloat16),
        in_specs=[hbm] * 5,
        out_specs=vmem,
        scratch_shapes=[
            pltpu.SMEM(tile_mask.shape, jnp.int32),
            pltpu.SMEM(dest.shape, jnp.int32),
            pltpu.VMEM(three_center.shape, jnp.bfloat16),
            pltpu.VMEM(tau_weights.shape, jnp.float32),
            pltpu.SemaphoreType.DMA((5,)),
        ],
        compiler_params=pltpu.CompilerParams(vmem_limit_bytes=56 * MIB),
        name="pack",
    )(tile_mask, dest, three_center, tau_weights, metric_half)
    masked, tau = pl.pallas_call(
        local_kernel,
        out_shape=(
            jax.ShapeDtypeStruct((local_rows, contracted), jnp.bfloat16),
            jax.ShapeDtypeStruct((1, contracted), jnp.float32),
        ),
        in_specs=[smem, vmem, vmem],
        out_specs=(vmem, vmem),
        compiler_params=pltpu.CompilerParams(vmem_limit_bytes=4 * MIB),
        name="local",
    )(*after((tile_mask, three_center, tau_weights), own))
    layer = lax.axis_index("row") // LAYER

    def early(group, masked):
        used = [got[m] for m in group]
        return pl.pallas_call(
            functools.partial(early_kernel, [len(piece) for piece in used]),
            out_shape=(
                jax.ShapeDtypeStruct((len(group), BLOCK, BLOCK), jnp.bfloat16),
                jax.ShapeDtypeStruct((len(group), rows, contracted), jnp.float32),
                jax.ShapeDtypeStruct((len(group), contracted, BLOCK), jnp.bfloat16),
            ),
            in_specs=[vmem] * (1 + sum(len(piece) for piece in used)),
            out_specs=(vmem, vmem, vmem),
            compiler_params=pltpu.CompilerParams(vmem_limit_bytes=8 * MIB),
            name="early",
        )(masked, *[part for piece in used for part in piece])

    def swap(piece, mask):
        return tuple(lax.ppermute(part, "row", [(i, i ^ mask) for i in range(devices)]) for part in piece)

    far = list(range(LAYER, devices, LAYER))
    near, inner, last = far[0], far[1:-1], far[-1]
    got = {0: (own,)}
    for mask in inner:
        got[mask] = swap(got[0], mask)
    got[near], got[2] = swap(got[0], near), swap(got[0], 2)
    got[near + 2], got[1] = swap(got[near], 2), swap(got[0], 1)
    got[3], got[near + 1] = swap(got[2], 1), swap(got[near], 1)
    first = [0, 1, 3, *inner, near + 2, near + 1]
    results = [early(first, after(masked, got[2]))]
    got[near + 3] = swap(after(got[near + 2], results[0]), 1)
    for mask in inner:
        got[mask + 1] = swap(after(got[mask], results[0]), 1)
    for mask in inner:
        got[mask + 2] = swap(after(got[mask], got[near], got[2], got[near + 1]), 2)
    for mask in inner:
        got[mask + 3] = swap(after(got[mask + 2], results[0], got[1], got[near]), 1)
    if len(far) == 3:
        middle = (layer == 1) | (layer == 2)
        onward = (2, 0, 3, 1)
        got[last] = (
            lax.ppermute(
                jnp.where(middle, got[2 * LAYER][0], got[near][0]),
                "row",
                [(i, onward[i // LAYER] * LAYER + i % LAYER) for i in range(devices)],
            ),
        )
    else:
        got[last] = swap(got[0], last)
    got[last + 1] = swap(after(got[last], results[0]), 1)
    got[last + 2] = swap(after(got[last], results[0]), 2)
    got[last + 3] = swap(after(got[last + 2], [got[mask] for mask in inner]), 1)
    second = [2, near] + [mask + 3 for mask in inner]
    groups = [first, second]
    results.append(early(second, masked))
    parts = [len(got[m]) for m in range(devices)]
    pieces = [part for m in range(devices) for part in got[m]]
    return pl.pallas_call(
        functools.partial(last_kernel, devices, groups, parts),
        out_shape=(
            jax.ShapeDtypeStruct((1, fanout, BLOCK, BLOCK), jnp.bfloat16),
            jax.ShapeDtypeStruct((rows, BLOCK), jnp.float32),
        ),
        in_specs=[hbm] + [vmem] * (2 + len(pieces) + 3 * len(groups)),
        out_specs=(hbm, vmem),
        scratch_shapes=[
            pltpu.VMEM((devices, BLOCK, BLOCK), jnp.bfloat16),
            pltpu.VMEM((BLOCK, contracted), jnp.float32),
            pltpu.VMEM((devices - sum(len(group) for group in groups), contracted, BLOCK), jnp.bfloat16),
            pltpu.VMEM((BLOCK, BLOCK), jnp.float32),
            pltpu.SMEM(dest.shape, jnp.int32),
            pltpu.SemaphoreType.DMA((fanout,)),
            pltpu.SemaphoreType.DMA,
        ],
        compiler_params=pltpu.CompilerParams(vmem_limit_bytes=24 * MIB),
        name="last",
    )(dest, masked, tau, *pieces, *[part for result in results for part in result])


def solution(mesh):
    return jax.shard_map(
        body,
        mesh=mesh,
        in_specs=(
            P(("groups", "row"), None),
            P("groups"),
            P("row", None),
            P("row", None),
            P("row", None),
        ),
        out_specs=(P(("groups", "row"), None, None, None), P(("groups", "row"), None)),
        check_vma=False,
    )
```

```python
import functools

import jax
import jax.numpy as jnp
from jax import lax
from jax.experimental import pallas as pl
from jax.experimental.pallas import tpu as pltpu
from jax.sharding import PartitionSpec as P

BLOCK = 128
LIST_ROWS = 16
LAYER = 4
CUT = 4 * BLOCK
MIB = 1 << 20
NT_DIMS = (((1,), (1,)), ((), ()))
NN_DIMS = (((1,), (0,)), ((), ()))
TN_DIMS = (((0,), (0,)), ((), ()))


def dot(a, b, dims=NN_DIMS):
    return lax.dot_general(a, b, dims, preferred_element_type=jnp.float32)


def split(x):
    high = x.astype(jnp.bfloat16)
    return high, (x - high.astype(jnp.float32)).astype(jnp.bfloat16)


def pack_kernel(
    mask_hbm, dest_hbm, rows_hbm, tau_hbm, metric_hbm, piece_ref, mask_ref, dest_ref, rows_ref, tau_ref, sems
):
    tiles = mask_ref.shape[1]
    depth = tiles * BLOCK
    moves = [
        (rows_hbm, rows_ref),
        (tau_hbm, tau_ref),
        (mask_hbm, mask_ref),
        (dest_hbm, dest_ref),
        (metric_hbm, piece_ref.at[depth : depth + BLOCK]),
    ]
    copies = [pltpu.make_async_copy(source, target, sems.at[k]) for k, (source, target) in enumerate(moves)]
    for copy in copies:
        copy.start()
    for copy in copies:
        copy.wait()
    tau = tau_ref[...].reshape(1, depth)
    for t in range(tiles):
        cols = slice(t * BLOCK, (t + 1) * BLOCK)
        weight = tau[:, cols] * mask_ref[0, t].astype(jnp.float32)
        piece_ref[cols, :] = (rows_ref[:, cols].astype(jnp.float32) * weight).astype(jnp.bfloat16)
    lane = lax.broadcasted_iota(jnp.int32, (LIST_ROWS, BLOCK), 1)
    listed = jnp.zeros((LIST_ROWS, BLOCK), jnp.float32)
    for j in range(dest_ref.shape[1]):
        listed += (lane == dest_ref[0, j]).astype(jnp.float32)
    piece_ref[depth + BLOCK :, :] = listed.astype(jnp.bfloat16)


def local_kernel(mask_ref, rows_ref, tau_ref, masked_ref, row_ref):
    row_ref[...] = tau_ref[...].reshape(row_ref.shape)
    for t in range(mask_ref.shape[1]):
        cols = slice(t * BLOCK, (t + 1) * BLOCK)
        masked_ref[:, cols] = rows_ref[:, cols] * mask_ref[0, t].astype(jnp.bfloat16)


def rows_of(piece, first, count):
    for part in piece:
        if first < part.shape[0]:
            return part[first : first + count, :]
        first -= part.shape[0]


def scaled_of(piece):
    depth = sum(part.shape[0] for part in piece) - BLOCK - LIST_ROWS
    return jnp.concatenate([rows_of(piece, t, BLOCK) for t in range(0, depth, BLOCK)], axis=1)


def metric_of(piece):
    depth = sum(part.shape[0] for part in piece) - BLOCK - LIST_ROWS
    return rows_of(piece, depth, BLOCK)


def listed_of(piece):
    part = piece[-1]
    return part[part.shape[0] - LIST_ROWS :, :]


def grouped(refs, parts):
    pieces = []
    for count in parts:
        pieces.append(tuple(refs[:count]))
        refs = refs[count:]
    return pieces


def strips_of(masked, pieces, strips):
    for k, piece in enumerate(pieces):
        strips[k][...] = dot(masked, scaled_of(piece), NT_DIMS).astype(jnp.bfloat16)


def window_of(me, pieces, windows, grams):
    rows = windows[0].shape[0]
    lane = lax.broadcasted_iota(jnp.int32, (rows, BLOCK), 1)
    row = lax.broadcasted_iota(jnp.int32, (rows, BLOCK), 0)
    pick = (lane == row + me * rows).astype(jnp.bfloat16)
    own = [dot(pick, metric_of(piece), NT_DIMS).astype(jnp.bfloat16) for piece in pieces]
    for k, piece in enumerate(pieces):
        windows[k][...] = dot(own[k], scaled_of(piece))
    for k, piece in enumerate(pieces):
        grams[k][...] = dot(scaled_of(piece), metric_of(piece), TN_DIMS).astype(jnp.bfloat16)


def early_kernel(parts, masked_ref, *refs):
    strips, windows, grams = refs[-3:]
    pieces = grouped(refs[:-3], parts)
    each = range(len(pieces))
    strips_of(masked_ref[...], pieces, [strips.at[k] for k in each])
    window_of(lax.axis_index("row"), pieces, [windows.at[k] for k in each], [grams.at[k] for k in each])


def last_kernel(devices, groups, parts, dest_hbm, masked_ref, tau_ref, *refs):
    pieces = grouped(refs, parts)
    early = refs[sum(parts) : sum(parts) + 3 * len(groups)]
    chi_ref, sand_ref, strips, window, late_grams, listed, dest_ref, sems, dest_sem = refs[
        sum(parts) + 3 * len(groups) :
    ]
    fetch = pltpu.make_async_copy(dest_hbm, dest_ref, dest_sem)
    fetch.start()
    me = lax.axis_index("row")
    rows = BLOCK // devices
    fanout = dest_ref.shape[1]
    late = [m for m in range(devices) if all(m not in group for group in groups)]
    strips_of(masked_ref[...], [pieces[m] for m in late], [strips.at[m] for m in late])
    grams = {m: late_grams.at[k] for k, m in enumerate(late)}
    for group, strip, part, gram in zip(groups, early[::3], early[1::3], early[2::3]):
        for k, m in enumerate(group):
            strips[m] = strip[k]
            window[m * rows : (m + 1) * rows, :] = part[k]
            grams[m] = gram.at[k]
    window_of(
        me,
        [pieces[m] for m in late],
        [window.at[m * rows : (m + 1) * rows] for m in late],
        [grams[m] for m in late],
    )

    for m in range(devices):
        entry = listed_of(pieces[m]).astype(jnp.float32)
        listed[m * rows : (m + 1) * rows, :] = entry[:rows, :]
    row = lax.broadcasted_iota(jnp.int32, (BLOCK, BLOCK), 0)
    column = lax.broadcasted_iota(jnp.int32, (BLOCK, BLOCK), 1)
    by_piece = (row == (column // rows ^ me)).astype(jnp.bfloat16)
    routes = dot(listed[...].astype(jnp.bfloat16), by_piece)
    same = row % rows == column % rows
    pair = jnp.where(same, routes + routes.T, 0.0).astype(jnp.bfloat16)
    mixed = dot(jnp.concatenate([pair, pair], axis=1), jnp.concatenate(split(window[...]), axis=0))
    fetch.wait()
    copies = [
        pltpu.make_async_copy(strips.at[dest_ref[0, j] ^ me], chi_ref.at[0, j], sems.at[j])
        for j in range(fanout)
    ]
    for copy in copies:
        copy.start()
    high, low = split(mixed / tau_ref[...])
    total = jnp.zeros((2 * rows, BLOCK), jnp.float32)
    for m in range(devices):
        part = slice(m * rows, (m + 1) * rows)
        total += dot(jnp.concatenate([high[part], low[part]], axis=0), grams[m][...])
    sand_ref[...] = total[:rows] + total[rows:]
    for copy in copies:
        copy.wait()


def after(value, *others):
    return lax.optimization_barrier((value, others))[0]


def body(three_center, tau_weights, tile_mask, dest, metric_half):
    devices = lax.axis_size("row")
    local_rows, contracted = three_center.shape
    fanout = dest.shape[1]
    rows = BLOCK // devices
    piece_rows = contracted + BLOCK + LIST_ROWS
    smem = pl.BlockSpec(memory_space=pltpu.SMEM)
    vmem = pl.BlockSpec(memory_space=pltpu.VMEM)
    hbm = pl.BlockSpec(memory_space=pltpu.HBM)
    own = pl.pallas_call(
        pack_kernel,
        out_shape=jax.ShapeDtypeStruct((piece_rows, BLOCK), jnp.bfloat16),
        in_specs=[hbm] * 5,
        out_specs=vmem,
        scratch_shapes=[
            pltpu.SMEM(tile_mask.shape, jnp.int32),
            pltpu.SMEM(dest.shape, jnp.int32),
            pltpu.VMEM(three_center.shape, jnp.bfloat16),
            pltpu.VMEM(tau_weights.shape, jnp.float32),
            pltpu.SemaphoreType.DMA((5,)),
        ],
        compiler_params=pltpu.CompilerParams(vmem_limit_bytes=56 * MIB),
        name="pack",
    )(tile_mask, dest, three_center, tau_weights, metric_half)
    masked, tau = pl.pallas_call(
        local_kernel,
        out_shape=(
            jax.ShapeDtypeStruct((local_rows, contracted), jnp.bfloat16),
            jax.ShapeDtypeStruct((1, contracted), jnp.float32),
        ),
        in_specs=[smem, vmem, vmem],
        out_specs=(vmem, vmem),
        compiler_params=pltpu.CompilerParams(vmem_limit_bytes=4 * MIB),
        name="local",
    )(*after((tile_mask, three_center, tau_weights), own))
    layer = lax.axis_index("row") // LAYER

    def early(group, masked):
        used = [got[m] for m in group]
        return pl.pallas_call(
            functools.partial(early_kernel, [len(piece) for piece in used]),
            out_shape=(
                jax.ShapeDtypeStruct((len(group), BLOCK, BLOCK), jnp.bfloat16),
                jax.ShapeDtypeStruct((len(group), rows, contracted), jnp.float32),
                jax.ShapeDtypeStruct((len(group), contracted, BLOCK), jnp.bfloat16),
            ),
            in_specs=[vmem] * (1 + sum(len(piece) for piece in used)),
            out_specs=(vmem, vmem, vmem),
            compiler_params=pltpu.CompilerParams(vmem_limit_bytes=8 * MIB),
            name="early",
        )(masked, *[part for piece in used for part in piece])

    def swap(piece, mask):
        return tuple(lax.ppermute(part, "row", [(i, i ^ mask) for i in range(devices)]) for part in piece)

    far = list(range(LAYER, devices, LAYER))
    near, inner, last = far[0], far[1:-1], far[-1]
    got = {0: (own,)}
    for mask in inner:
        got[mask] = swap(got[0], mask)
    got[near], got[2] = swap(got[0], near), swap(got[0], 2)
    got[near + 2], got[1] = swap(got[near], 2), swap(got[0], 1)
    got[3], got[near + 1] = swap(got[2], 1), swap(got[near], 1)
    first = [0, 1, 3, *inner, near + 2, near + 1]
    results = [early(first, after(masked, got[2]))]
    got[near + 3] = swap(after(got[near + 2], results[0]), 1)
    for mask in inner:
        got[mask + 1] = swap(got[mask], 1)
    for mask in inner:
        got[mask + 2] = swap(after(got[mask], got[near], got[2], got[near + 1]), 2)
    for mask in inner:
        got[mask + 3] = swap(after(got[mask + 2], results[0], got[1], got[near]), 1)
    if len(far) == 3:
        middle = (layer == 1) | (layer == 2)
        onward = (2, 0, 3, 1)
        got[last] = (
            lax.ppermute(
                jnp.where(middle, got[2 * LAYER][0], got[near][0]),
                "row",
                [(i, onward[i // LAYER] * LAYER + i % LAYER) for i in range(devices)],
            ),
        )
    else:
        got[last] = swap(got[0], last)
    got[last + 1] = swap(after(got[last], results[0]), 1)
    got[last + 2] = swap(after(got[last], results[0]), 2)
    got[last + 3] = swap(after(got[last + 2], [got[mask] for mask in inner]), 1)
    second = [2, near]
    for mask in inner:
        second += [mask + 1, mask + 3]
    second += [last + 1, near + 3]
    groups = [first, second]
    results.append(early(second, masked))
    parts = [len(got[m]) for m in range(devices)]
    pieces = [part for m in range(devices) for part in got[m]]
    return pl.pallas_call(
        functools.partial(last_kernel, devices, groups, parts),
        out_shape=(
            jax.ShapeDtypeStruct((1, fanout, BLOCK, BLOCK), jnp.bfloat16),
            jax.ShapeDtypeStruct((rows, BLOCK), jnp.float32),
        ),
        in_specs=[hbm] + [vmem] * (2 + len(pieces) + 3 * len(groups)),
        out_specs=(hbm, vmem),
        scratch_shapes=[
            pltpu.VMEM((devices, BLOCK, BLOCK), jnp.bfloat16),
            pltpu.VMEM((BLOCK, contracted), jnp.float32),
            pltpu.VMEM((devices - sum(len(group) for group in groups), contracted, BLOCK), jnp.bfloat16),
            pltpu.VMEM((BLOCK, BLOCK), jnp.float32),
            pltpu.SMEM(dest.shape, jnp.int32),
            pltpu.SemaphoreType.DMA((fanout,)),
            pltpu.SemaphoreType.DMA,
        ],
        compiler_params=pltpu.CompilerParams(vmem_limit_bytes=24 * MIB),
        name="last",
    )(dest, masked, tau, *pieces, *[part for result in results for part in result])


def solution(mesh):
    return jax.shard_map(
        body,
        mesh=mesh,
        in_specs=(
            P(("groups", "row"), None),
            P("groups"),
            P("row", None),
            P("row", None),
            P("row", None),
        ),
        out_specs=(P(("groups", "row"), None, None, None), P(("groups", "row"), None)),
        check_vma=False,
    )
```

```python
import functools

import jax
import jax.numpy as jnp
from jax import lax
from jax.experimental import pallas as pl
from jax.experimental.pallas import tpu as pltpu
from jax.sharding import PartitionSpec as P

BLOCK = 128
LIST_ROWS = 16
LAYER = 4
CUT = 4 * BLOCK
MIB = 1 << 20
NT_DIMS = (((1,), (1,)), ((), ()))
NN_DIMS = (((1,), (0,)), ((), ()))
TN_DIMS = (((0,), (0,)), ((), ()))


def dot(a, b, dims=NN_DIMS):
    return lax.dot_general(a, b, dims, preferred_element_type=jnp.float32)


def split(x):
    high = x.astype(jnp.bfloat16)
    return high, (x - high.astype(jnp.float32)).astype(jnp.bfloat16)


def pack_kernel(
    mask_hbm, dest_hbm, rows_hbm, tau_hbm, metric_hbm, piece_ref, mask_ref, dest_ref, rows_ref, tau_ref, sems
):
    tiles = mask_ref.shape[1]
    depth = tiles * BLOCK
    moves = [
        (rows_hbm, rows_ref),
        (tau_hbm, tau_ref),
        (mask_hbm, mask_ref),
        (dest_hbm, dest_ref),
        (metric_hbm, piece_ref.at[depth : depth + BLOCK]),
    ]
    copies = [pltpu.make_async_copy(source, target, sems.at[k]) for k, (source, target) in enumerate(moves)]
    for copy in copies:
        copy.start()
    rows_copy, tau_copy, mask_copy, dest_copy, metric_copy = copies
    dest_copy.wait()
    lane = lax.broadcasted_iota(jnp.int32, (LIST_ROWS, BLOCK), 1)
    listed = jnp.zeros((LIST_ROWS, BLOCK), jnp.float32)
    for j in range(dest_ref.shape[1]):
        listed += (lane == dest_ref[0, j]).astype(jnp.float32)
    piece_ref[depth + BLOCK :, :] = listed.astype(jnp.bfloat16)
    for copy in (mask_copy, tau_copy, rows_copy):
        copy.wait()
    tau = tau_ref[...].reshape(1, depth)
    for t in range(tiles):
        cols = slice(t * BLOCK, (t + 1) * BLOCK)
        weight = tau[:, cols] * mask_ref[0, t].astype(jnp.float32)
        piece_ref[cols, :] = (rows_ref[:, cols].astype(jnp.float32) * weight).astype(jnp.bfloat16)
    metric_copy.wait()


def local_kernel(mask_ref, rows_ref, tau_ref, masked_ref, row_ref):
    row_ref[...] = tau_ref[...].reshape(row_ref.shape)
    for t in range(mask_ref.shape[1]):
        cols = slice(t * BLOCK, (t + 1) * BLOCK)
        masked_ref[:, cols] = rows_ref[:, cols] * mask_ref[0, t].astype(jnp.bfloat16)


def rows_of(piece, first, count):
    for part in piece:
        if first < part.shape[0]:
            return part[first : first + count, :]
        first -= part.shape[0]


def scaled_of(piece):
    depth = sum(part.shape[0] for part in piece) - BLOCK - LIST_ROWS
    return jnp.concatenate([rows_of(piece, t, BLOCK) for t in range(0, depth, BLOCK)], axis=1)


def metric_of(piece):
    depth = sum(part.shape[0] for part in piece) - BLOCK - LIST_ROWS
    return rows_of(piece, depth, BLOCK)


def listed_of(piece):
    part = piece[-1]
    return part[part.shape[0] - LIST_ROWS :, :]


def grouped(refs, parts):
    pieces = []
    for count in parts:
        pieces.append(tuple(refs[:count]))
        refs = refs[count:]
    return pieces


def strips_of(masked, pieces, strips):
    for k, piece in enumerate(pieces):
        strips[k][...] = dot(masked, scaled_of(piece), NT_DIMS).astype(jnp.bfloat16)


def window_of(me, pieces, windows, grams):
    rows = windows[0].shape[0]
    lane = lax.broadcasted_iota(jnp.int32, (rows, BLOCK), 1)
    row = lax.broadcasted_iota(jnp.int32, (rows, BLOCK), 0)
    pick = (lane == row + me * rows).astype(jnp.bfloat16)
    own = [dot(pick, metric_of(piece), NT_DIMS).astype(jnp.bfloat16) for piece in pieces]
    for k, piece in enumerate(pieces):
        windows[k][...] = dot(own[k], scaled_of(piece))
    for k, piece in enumerate(pieces):
        grams[k][...] = dot(scaled_of(piece), metric_of(piece), TN_DIMS).astype(jnp.bfloat16)


def early_kernel(parts, masked_ref, *refs):
    strips, windows, grams = refs[-3:]
    pieces = grouped(refs[:-3], parts)
    each = range(len(pieces))
    strips_of(masked_ref[...], pieces, [strips.at[k] for k in each])
    window_of(lax.axis_index("row"), pieces, [windows.at[k] for k in each], [grams.at[k] for k in each])


def last_kernel(devices, groups, parts, dest_hbm, masked_ref, tau_ref, *refs):
    pieces = grouped(refs, parts)
    early = refs[sum(parts) : sum(parts) + 3 * len(groups)]
    chi_ref, sand_ref, strips, window, late_grams, listed, dest_ref, sems, dest_sem = refs[
        sum(parts) + 3 * len(groups) :
    ]
    fetch = pltpu.make_async_copy(dest_hbm, dest_ref, dest_sem)
    fetch.start()
    me = lax.axis_index("row")
    rows = BLOCK // devices
    fanout = dest_ref.shape[1]
    late = [m for m in range(devices) if all(m not in group for group in groups)]
    strips_of(masked_ref[...], [pieces[m] for m in late], [strips.at[m] for m in late])
    grams = {m: late_grams.at[k] for k, m in enumerate(late)}
    for group, strip, part, gram in zip(groups, early[::3], early[1::3], early[2::3]):
        for k, m in enumerate(group):
            strips[m] = strip[k]
            window[m * rows : (m + 1) * rows, :] = part[k]
            grams[m] = gram.at[k]
    window_of(
        me,
        [pieces[m] for m in late],
        [window.at[m * rows : (m + 1) * rows] for m in late],
        [grams[m] for m in late],
    )

    for m in range(devices):
        entry = listed_of(pieces[m]).astype(jnp.float32)
        listed[m * rows : (m + 1) * rows, :] = entry[:rows, :]
    row = lax.broadcasted_iota(jnp.int32, (BLOCK, BLOCK), 0)
    column = lax.broadcasted_iota(jnp.int32, (BLOCK, BLOCK), 1)
    by_piece = (row == (column // rows ^ me)).astype(jnp.bfloat16)
    routes = dot(listed[...].astype(jnp.bfloat16), by_piece)
    same = row % rows == column % rows
    pair = jnp.where(same, routes + routes.T, 0.0).astype(jnp.bfloat16)
    mixed = dot(jnp.concatenate([pair, pair], axis=1), jnp.concatenate(split(window[...]), axis=0))
    fetch.wait()
    copies = [
        pltpu.make_async_copy(strips.at[dest_ref[0, j] ^ me], chi_ref.at[0, j], sems.at[j])
        for j in range(fanout)
    ]
    for copy in copies:
        copy.start()
    high, low = split(mixed / tau_ref[...])
    total = jnp.zeros((2 * rows, BLOCK), jnp.float32)
    for m in range(devices):
        part = slice(m * rows, (m + 1) * rows)
        total += dot(jnp.concatenate([high[part], low[part]], axis=0), grams[m][...])
    sand_ref[...] = total[:rows] + total[rows:]
    for copy in copies:
        copy.wait()


def after(value, *others):
    return lax.optimization_barrier((value, others))[0]


def body(three_center, tau_weights, tile_mask, dest, metric_half):
    devices = lax.axis_size("row")
    local_rows, contracted = three_center.shape
    fanout = dest.shape[1]
    rows = BLOCK // devices
    piece_rows = contracted + BLOCK + LIST_ROWS
    smem = pl.BlockSpec(memory_space=pltpu.SMEM)
    vmem = pl.BlockSpec(memory_space=pltpu.VMEM)
    hbm = pl.BlockSpec(memory_space=pltpu.HBM)
    own = pl.pallas_call(
        pack_kernel,
        out_shape=jax.ShapeDtypeStruct((piece_rows, BLOCK), jnp.bfloat16),
        in_specs=[hbm] * 5,
        out_specs=vmem,
        scratch_shapes=[
            pltpu.SMEM(tile_mask.shape, jnp.int32),
            pltpu.SMEM(dest.shape, jnp.int32),
            pltpu.VMEM(three_center.shape, jnp.bfloat16),
            pltpu.VMEM(tau_weights.shape, jnp.float32),
            pltpu.SemaphoreType.DMA((5,)),
        ],
        compiler_params=pltpu.CompilerParams(vmem_limit_bytes=56 * MIB),
        name="pack",
    )(tile_mask, dest, three_center, tau_weights, metric_half)
    masked, tau = pl.pallas_call(
        local_kernel,
        out_shape=(
            jax.ShapeDtypeStruct((local_rows, contracted), jnp.bfloat16),
            jax.ShapeDtypeStruct((1, contracted), jnp.float32),
        ),
        in_specs=[smem, vmem, vmem],
        out_specs=(vmem, vmem),
        compiler_params=pltpu.CompilerParams(vmem_limit_bytes=4 * MIB),
        name="local",
    )(*after((tile_mask, three_center, tau_weights), own))
    layer = lax.axis_index("row") // LAYER

    def early(group, masked):
        used = [got[m] for m in group]
        return pl.pallas_call(
            functools.partial(early_kernel, [len(piece) for piece in used]),
            out_shape=(
                jax.ShapeDtypeStruct((len(group), BLOCK, BLOCK), jnp.bfloat16),
                jax.ShapeDtypeStruct((len(group), rows, contracted), jnp.float32),
                jax.ShapeDtypeStruct((len(group), contracted, BLOCK), jnp.bfloat16),
            ),
            in_specs=[vmem] * (1 + sum(len(piece) for piece in used)),
            out_specs=(vmem, vmem, vmem),
            compiler_params=pltpu.CompilerParams(vmem_limit_bytes=8 * MIB),
            name="early",
        )(masked, *[part for piece in used for part in piece])

    def swap(piece, mask):
        return tuple(lax.ppermute(part, "row", [(i, i ^ mask) for i in range(devices)]) for part in piece)

    far = list(range(LAYER, devices, LAYER))
    near, inner, last = far[0], far[1:-1], far[-1]
    got = {0: (own,)}
    for mask in inner:
        got[mask] = swap(got[0], mask)
    got[near], got[2] = swap(got[0], near), swap(got[0], 2)
    got[near + 2], got[1] = swap(got[near], 2), swap(got[0], 1)
    got[3], got[near + 1] = swap(got[2], 1), swap(got[near], 1)
    first = [0, 1, 3, *inner, near + 2, near + 1]
    results = [early(first, after(masked, got[2]))]
    got[near + 3] = swap(after(got[near + 2], results[0]), 1)
    for mask in inner:
        got[mask + 1] = swap(got[mask], 1)
    for mask in inner:
        got[mask + 2] = swap(after(got[mask], got[near], got[2], got[near + 1]), 2)
    for mask in inner:
        got[mask + 3] = swap(after(got[mask + 2], results[0], got[1], got[near]), 1)
    if len(far) == 3:
        middle = (layer == 1) | (layer == 2)
        onward = (2, 0, 3, 1)
        got[last] = (
            lax.ppermute(
                jnp.where(middle, got[2 * LAYER][0], got[near][0]),
                "row",
                [(i, onward[i // LAYER] * LAYER + i % LAYER) for i in range(devices)],
            ),
        )
    else:
        got[last] = swap(got[0], last)
    got[last + 1] = swap(after(got[last], results[0]), 1)
    got[last + 2] = swap(after(got[last], results[0]), 2)
    got[last + 3] = swap(after(got[last + 2], [got[mask] for mask in inner]), 1)
    second = [2, near]
    for mask in inner:
        second += [mask + 1, mask + 3]
    second += [last + 1, near + 3]
    groups = [first, second]
    results.append(early(second, masked))
    parts = [len(got[m]) for m in range(devices)]
    pieces = [part for m in range(devices) for part in got[m]]
    return pl.pallas_call(
        functools.partial(last_kernel, devices, groups, parts),
        out_shape=(
            jax.ShapeDtypeStruct((1, fanout, BLOCK, BLOCK), jnp.bfloat16),
            jax.ShapeDtypeStruct((rows, BLOCK), jnp.float32),
        ),
        in_specs=[hbm] + [vmem] * (2 + len(pieces) + 3 * len(groups)),
        out_specs=(hbm, vmem),
        scratch_shapes=[
            pltpu.VMEM((devices, BLOCK, BLOCK), jnp.bfloat16),
            pltpu.VMEM((BLOCK, contracted), jnp.float32),
            pltpu.VMEM((devices - sum(len(group) for group in groups), contracted, BLOCK), jnp.bfloat16),
            pltpu.VMEM((BLOCK, BLOCK), jnp.float32),
            pltpu.SMEM(dest.shape, jnp.int32),
            pltpu.SemaphoreType.DMA((fanout,)),
            pltpu.SemaphoreType.DMA,
        ],
        compiler_params=pltpu.CompilerParams(vmem_limit_bytes=24 * MIB),
        name="last",
    )(dest, masked, tau, *pieces, *[part for result in results for part in result])


def solution(mesh):
    return jax.shard_map(
        body,
        mesh=mesh,
        in_specs=(
            P(("groups", "row"), None),
            P("groups"),
            P("row", None),
            P("row", None),
            P("row", None),
        ),
        out_specs=(P(("groups", "row"), None, None, None), P(("groups", "row"), None)),
        check_vma=False,
    )
```
